32 devices in a mesh: dp: 4 (over z), expert: 4 (over y, core), mp: 2 (over x).
Axes of the slice: x: 2, y: 2, z: 4, core: 2. Of those that a mesh axis runs over, the one named last changes fastest.
Arguments:
- hidden: bfloat16 [2048, 2048], P(('dp', 'expert', 'mp')), may hold values from -6 to 6
- norm_gain: float32 [2048], replicated, may hold values from 0.1 to 1.9
- expert_in: float32 [16, 2048, 2816], P('dp', ('expert', 'mp')), may hold values from -0.125 to 0.125
- expert_out: float32 [16, 2048, 1408], P('dp', ('expert', 'mp')), may hold values from -0.15625 to 0.15625
- expert_ids: int32 [2048, 6], P(('dp', 'expert', 'mp')), may hold values from 0 to 15, all different within a row; in each aligned block of 64 rows (0 to 63, 64 to 127, ...) at most 48 rows name the same one
- gate_levels: int32 [2048, 6], P(('dp', 'expert', 'mp')), may hold values from 1 to 255
- shared_gate: bfloat16 [2048, 2816], P(('dp', 'expert'), 'mp'), may hold values from -0.125 to 0.125
- shared_up: bfloat16 [2048, 2816], P(('dp', 'expert'), 'mp'), may hold values from -0.125 to 0.125
- shared_down: bfloat16 [2048, 2816], P(('dp', 'expert'), 'mp'), may hold values from -0.109375 to 0.109375
- next_gain: float32 [2048], replicated, may hold values from 0.1 to 1.9
- kv_weight: bfloat16 [2048, 576], P(None, 'mp'), may hold values from -0.125 to 0.125
Outputs:
- layer_out: bfloat16 [2048, 2048], P(('dp', 'expert', 'mp'))
- kv_latent: bfloat16 [2048, 576], P(('dp', 'expert'), 'mp')
The draws below stay inside these ranges and needn't reach their ends.
Inputs may be any that keep to these rules, and one draw needn't show every extreme that they name: `expert_ids`: each row names 6 different experts. Among the 64 rows of one device no expert is named by more than 48 rows, and in every draw some expert is named by exactly 48 rows of some device.
All inputs are finite; a program needn't handle non-finite values.
Results may differ from the reference program's by a relative error of at most 0.012.
Values may be sent and summed in bfloat16 or wider, within the bound.
A program may use at most 128 MiB of HBM per device.

```python
import math
import jax
import jax.numpy as jnp
import numpy as np
from jax import lax

D = 2048
FF = 1408
SFF = 2816
KV = 576
TOPK = 6
TOK_DEV = 64
EXPERTS = 16
CAP = 48
TOKENS = 2048
N_MP = 2


def plant(values, key, low, largest):
    index_at = [jax.random.randint(jax.random.fold_in(key, axis), (), 0, length) for axis, length in enumerate(values.shape)]
    main_axis = values.shape.index(max(values.shape))
    beside = index_at[:main_axis] + [(index_at[main_axis] + 1) % values.shape[main_axis]] + index_at[main_axis + 1:]
    return values.at[tuple(index_at)].set(low).at[tuple(beside)].set(largest)


def block_scale(key, shape, cuts, smallest, top_value):
    level = 1.0
    for dim, blocks in cuts:
        draws = jax.random.uniform(jax.random.fold_in(jax.random.fold_in(key, 6), dim), (blocks,), jnp.float32, smallest / len(cuts), top_value / len(cuts))
        level = level * jnp.repeat(jnp.exp(draws), shape[dim] // blocks).reshape((-1,) + (1,) * (len(shape) - 1 - dim))
    return level


def routed_block(own_key, own, number, rows, number_of, top, reach, lean):
    sequence = jax.random.permutation(own_key, number_of)
    crowded, usual = load_shares(number_of, rows * top, reach, lean, True), load_shares(number_of, rows * top, reach, lean, False)
    places = jnp.arange(number_of)

    def named(lengths, rotation):
        used = int((lengths > 0).sum())
        fixed = max(1, used // 4)
        passed = fixed + (places - fixed + rotation * (used - fixed)) % max(1, number_of - fixed)
        return jnp.zeros((number_of,), jnp.int32).at[sequence[jnp.where(places < fixed, places, passed)]].set(jnp.asarray(lengths, jnp.int32))

    lengths = jnp.where(number % 4 == 0, named(crowded, number // 4), named(usual, number - number // 4 - 1))
    mixed = jax.random.permutation(jax.random.fold_in(own, 3), number_of)
    donor, taker = mixed[0:number_of // 2 * 2:2], mixed[1:number_of // 2 * 2:2]
    slack = jnp.minimum(lengths[donor] - 1, reach - lengths[taker]) // 2
    slack = jnp.where((donor == sequence[0]) | (taker == sequence[0]) | (lengths[taker] == 0), 0, jnp.maximum(slack, 0))
    passed = jax.random.randint(jax.random.fold_in(own, 4), (number_of // 2,), 0, 1 << 20) % (slack + 1)
    lengths = lengths.at[donor].add(-passed).at[taker].add(passed)
    items = jnp.searchsorted(jnp.cumsum(lengths), jnp.arange(rows * top), side="right").astype(jnp.int32)
    listing = items.reshape(top, rows).T
    listing = listing[jax.random.permutation(jax.random.fold_in(own, 1), rows)]
    rotation = jax.random.randint(jax.random.fold_in(own, 2), (rows, 1), 0, top)
    return jnp.take_along_axis(listing, (jnp.arange(top)[None, :] + rotation) % top, axis=1)


def load_shares(count, total, reach, lean, full):
    loads = [(1 << 20) // math.isqrt(grade ** lean) + 1 for grade in range(1, count + 1)]
    largest = reach if full else min(reach, max(-(-total // count), total * loads[0] // sum(loads)))
    least = 1 if total - largest >= count - 1 else 0
    given, spare = [largest] + [least] * (count - 1), total - largest - least * (count - 1)
    while spare > 0:
        candidates = [i for i in range(1, count) if given[i] < largest] or [i for i in range(1, count) if given[i] < reach]
        mass, left = sum([loads[i] for i in candidates]), spare
        for i in candidates:
            addition = min(reach - given[i], max(1, left * loads[i] // mass), spare)
            given[i] = given[i] + addition
            spare = spare - addition
    return np.array(given)


def scatter_about(rng, shape, width, limit, cuts=(), kind=jnp.bfloat16):
    entries = jax.random.normal(rng, shape, jnp.float32) * width
    if len(cuts) > 0:
        entries = block_scale(rng, shape, cuts, -0.22, 0.18) * entries
    return jnp.clip(entries, min=-limit, max=limit).astype(kind)


def setup_inputs(seed: int = 0) -> dict:
    arg_keys = jax.random.split(jax.random.key(seed), 12)
    hidden = scatter_about(arg_keys[0], (TOKENS, D), 1.0, 6.0, ((0, 32),))
    norm_gain = jnp.clip(1.0 + 0.18 * jax.random.normal(arg_keys[1], (D,), jnp.float32), 0.1, 1.9)
    expert_in = scatter_about(arg_keys[2], (EXPERTS, D, 2 * FF), D ** -0.5, 0.125, ((0, 4), (1, 8)), jnp.float32)
    expert_out = scatter_about(arg_keys[3], (EXPERTS, D, FF), FF ** -0.5, 0.15625, ((0, 4), (1, 8)), jnp.float32)
    expert_ids_keys = jax.random.split(jax.random.fold_in(arg_keys[4], 1), TOKENS // TOK_DEV)
    expert_ids_turns = jax.random.permutation(jax.random.fold_in(arg_keys[4], 3), TOKENS // TOK_DEV)
    expert_ids = jax.vmap(lambda own, number: routed_block(jax.random.fold_in(arg_keys[4], 2), own, number, TOK_DEV, EXPERTS, TOPK, CAP, 2))(expert_ids_keys, expert_ids_turns).reshape((TOKENS, TOPK))
    gate_levels = plant(jax.random.randint(arg_keys[5], (TOKENS, TOPK), 1, 256), jax.random.fold_in(arg_keys[5], 1), 1, 255).astype(jnp.int32)
    shared_gate = scatter_about(arg_keys[6], (D, SFF), D ** -0.5, 0.125, ((0, 16), (1, 2)))
    shared_up = scatter_about(arg_keys[7], (D, SFF), D ** -0.5, 0.125, ((0, 16), (1, 2)))
    shared_down = scatter_about(arg_keys[8], (D, SFF), SFF ** -0.5, 0.109375, ((0, 16), (1, 2)))
    next_gain = jnp.clip(1.0 + 0.18 * jax.random.normal(arg_keys[9], (D,), jnp.float32), 0.1, 1.9)
    kv_weight = scatter_about(arg_keys[10], (D, KV), D ** -0.5, 0.125, ((1, 2),))
    return {"hidden": hidden, "norm_gain": norm_gain, "expert_in": expert_in, "expert_out": expert_out, "expert_ids": expert_ids, "gate_levels": gate_levels, "shared_gate": shared_gate, "shared_up": shared_up, "shared_down": shared_down, "next_gain": next_gain, "kv_weight": kv_weight}


def rms_scale(values, gain):
    wide = values.astype(jnp.float32)
    mean_sq = lax.optimization_barrier(jnp.mean(wide * wide, axis=-1, keepdims=True))
    return (wide * lax.rsqrt(mean_sq + 1e-06) * gain).astype(jnp.bfloat16)

def expert_apply(rows, w_in, w_out):
    quarter = FF // N_MP
    gate_up = jnp.dot(rows, w_in, preferred_element_type=jnp.float32)
    act = (jax.nn.silu(gate_up[:, :FF]) * gate_up[:, FF:]).astype(jnp.bfloat16)
    total = jnp.zeros((rows.shape[0], rows.shape[1]), jnp.float32)
    for run in range(N_MP):
        part = lax.dot_general(act[:, run * quarter:(run + 1) * quarter], w_out[:, run * quarter:(run + 1) * quarter], (((1,), (1,)), ((), ())), preferred_element_type=jnp.float32)
        total = total + lax.optimization_barrier(part.astype(jnp.bfloat16)).astype(jnp.float32)
    return total.astype(jnp.bfloat16)

def reference(hidden, norm_gain, expert_in, expert_out, expert_ids, gate_levels, shared_gate, shared_up, shared_down, next_gain, kv_weight):
    normed = rms_scale(hidden, norm_gain)
    levels = gate_levels.astype(jnp.float32)
    gate_weights = levels / lax.optimization_barrier(jnp.sum(levels, axis=1, keepdims=True))
    pair_ids = expert_ids.reshape(-1)
    pair_token = (jnp.arange(TOKENS * TOPK, dtype=jnp.int32) // TOPK).astype(jnp.int32)
    buffer_rows = CAP * (TOKENS // TOK_DEV)

    def one_expert(routed, inputs):
        index, w_in, w_out = inputs
        member = pair_ids == index
        position = (jnp.cumsum(member.astype(jnp.int32)) - 1).astype(jnp.int32)
        target = jnp.where(member, position, buffer_rows).astype(jnp.int32)
        token_of_slot = jnp.zeros((buffer_rows,), jnp.int32).at[target].set(pair_token, mode='drop')
        rows = normed[token_of_slot]
        result = expert_apply(rows, w_in.astype(jnp.bfloat16), w_out.astype(jnp.bfloat16))
        member_pairs = member.reshape(TOKENS, TOPK)
        pos_pairs = jnp.where(member, position, 0).astype(jnp.int32).reshape(TOKENS, TOPK)
        for slot_k in range(TOPK):
            weight = jnp.where(member_pairs[:, slot_k], gate_weights[:, slot_k], 0.0)
            routed = routed + weight[:, None] * result[pos_pairs[:, slot_k]].astype(jnp.float32)
        return (routed, None)
    routed, _ = lax.scan(one_expert, jnp.zeros((TOKENS, D), jnp.float32), (jnp.arange(EXPERTS, dtype=jnp.int32), expert_in, expert_out))
    gate_part = jnp.dot(normed, shared_gate, preferred_element_type=jnp.float32)
    up_part = jnp.dot(normed, shared_up, preferred_element_type=jnp.float32)
    shared_act = (jax.nn.silu(gate_part) * up_part).astype(jnp.bfloat16)
    shared_out = lax.dot_general(shared_act, shared_down, (((1,), (1,)), ((), ())), preferred_element_type=jnp.float32)
    layer_out = (hidden.astype(jnp.float32) + routed + shared_out).astype(jnp.bfloat16)
    next_normed = rms_scale(layer_out, next_gain)
    kv_latent = jnp.dot(next_normed, kv_weight, preferred_element_type=jnp.float32).astype(jnp.bfloat16)
    return (layer_out, kv_latent)
```

```python
import functools

import jax
import jax.numpy as jnp
from jax import lax
from jax.experimental import pallas as pl
from jax.experimental.pallas import tpu as pltpu
from jax.sharding import PartitionSpec as P

MESH = pl.DeviceIdType.MESH
LANES = 128
VMEM_BYTES = 56 * 1024 * 1024


def position():
    return lax.axis_index("dp"), lax.axis_index("expert"), lax.axis_index("mp")


def barrier(peers):
    sem = pltpu.get_barrier_semaphore()
    for peer in peers:
        pl.semaphore_signal(sem, inc=1, device_id=peer, device_id_type=MESH)
    pl.semaphore_wait(sem, len(peers))


def pack_kernel(in_ref, out_ref, in_pack, out_pack):
    rows, full = out_ref.shape[1:]
    main = full // (2 * LANES) * LANES
    mid = main + LANES
    half = LANES // 2
    low = lax.broadcasted_iota(jnp.int32, (rows, LANES), 1) < half
    for first, core in ((0, 0), (mid, 1)):
        in_pack[core, :, :main] = in_ref[0, :, first : first + main].astype(jnp.bfloat16)
        in_pack[core, :, main : 2 * main] = in_ref[
            0, :, full + first : full + first + main
        ].astype(jnp.bfloat16)
        out_pack[core, :, :main] = out_ref[0, :, first : first + main].astype(jnp.bfloat16)
    gate = in_ref[0, :, main:mid]
    up = in_ref[0, :, full + main : full + mid]
    down = out_ref[0, :, main:mid]
    in_pack[0, :, 2 * main :] = jnp.where(low, gate, pltpu.roll(up, half, 1)).astype(jnp.bfloat16)
    in_pack[1, :, 2 * main :] = jnp.where(low, pltpu.roll(gate, half, 1), up).astype(jnp.bfloat16)
    out_pack[0, :, main:] = jnp.where(low, down, 0.0).astype(jnp.bfloat16)
    out_pack[1, :, main:] = jnp.where(low, pltpu.roll(down, half, 1), 0.0).astype(jnp.bfloat16)


def pack(expert_in, expert_out):
    local_e, rows, double = expert_in.shape
    full = double // 2
    wide = (full // (2 * LANES) + 1) * LANES
    tile = 128
    return pl.pallas_call(
        pack_kernel,
        grid=(local_e, rows // tile),
        in_specs=[
            pl.BlockSpec((1, tile, double), lambda e, i: (e, i, 0)),
            pl.BlockSpec((1, tile, full), lambda e, i: (e, i, 0)),
        ],
        out_specs=[
            pl.BlockSpec((2, tile, full), lambda e, i: (e, i, 0)),
            pl.BlockSpec((2, tile, wide), lambda e, i: (e, i, 0)),
        ],
        out_shape=[
            jax.ShapeDtypeStruct((2 * local_e, rows, full), jnp.bfloat16),
            jax.ShapeDtypeStruct((2 * local_e, rows, wide), jnp.bfloat16),
        ],
        compiler_params=pltpu.CompilerParams(vmem_limit_bytes=VMEM_BYTES),
    )(expert_in, expert_out)


def gather_kernel(
    n_dp, n_exp, tok, w_in, w_out, s_in, s_out, all_tok, gu, dn,
    z_s, z_r, h_s, h_r, f_s, f_r, win_s, win_r, wout_s, wout_r, sin_s, sin_r, sout_s, sout_r, local,
):
    dp, ex, mp = position()
    block = tok.shape[0]
    in_cols, out_cols = w_in.shape[2], w_out.shape[2]
    w_rows, s_rows = w_in.shape[1], s_in.shape[1]
    mate = (dp, ex + 1 - 2 * lax.rem(ex, 2), mp)
    xpeer = (dp, ex, 1 - mp)
    ypeer = (dp, lax.rem(ex + n_exp // 2, n_exp), mp)
    plane = [
        (a, b) for a in range(n_exp) for b in range(2) if (a, b) != (0, 0)
    ]
    column = [
        (a, b) for a in range(n_dp) for b in range(n_exp) if (a, b) != (0, 0)
    ]

    def in_plane(a, b):
        return (dp, lax.rem(ex + a, n_exp), lax.rem(mp + b, 2))

    def in_column(a, b):
        return (lax.rem(dp + a, n_dp), lax.rem(ex + b, n_exp), mp)

    barrier(
        [in_plane(a, b) for a, b in plane] + [in_column(a, b) for a, b in column if a != 0]
    )

    def rows_of(k, e, m):
        index = (lax.rem(dp + n_dp - k, n_dp) * n_exp + e) * 2 + m
        return pl.ds(pl.multiple_of(index * block, block), block)

    started = []

    def send(src, dst, s, r, to):
        copy = pltpu.make_async_remote_copy(
            src_ref=src, dst_ref=dst, send_sem=s, recv_sem=r, device_id=to, device_id_type=MESH
        )
        copy.start()
        started.append(copy)
        return copy

    mine = rows_of(0, ex, mp)
    from_z = {}
    for k in range(1, n_dp):
        from_z[k] = send(
            tok, all_tok.at[mine], z_s.at[k], z_r.at[k], (lax.rem(dp + k, n_dp), ex, mp)
        )
    own = pltpu.make_async_copy(tok, all_tok.at[mine], local.at[0])
    own.start()
    from_h = {}

    def spread(k, src):
        rows = rows_of(k, ex, mp)
        for way, to in enumerate((xpeer, ypeer, mate)):
            at = way * n_dp + k
            from_h[way, k] = send(src, all_tok.at[rows], h_s.at[at], h_r.at[at], to)

    spread(0, tok)

    w_at = pl.ds(pl.multiple_of((ex * 2 + mp) * w_rows, w_rows), w_rows)
    s_at = pl.ds(pl.multiple_of((dp * n_exp + ex) * s_rows, s_rows), s_rows)
    rest = []
    locals_ = [own]
    pieces = (
        (w_in, gu.at[w_at, pl.ds(0, in_cols)], ex * 2 + mp),
        (w_out, dn.at[w_at, pl.ds(0, out_cols)], ex * 2 + mp),
        (s_in, gu.at[s_at, pl.ds(in_cols, s_in.shape[2])], dp * n_exp + ex),
        (s_out, dn.at[s_at, pl.ds(out_cols, s_out.shape[2])], dp * n_exp + ex),
    )
    for at, (src, dst, index) in enumerate(pieces):
        copy = pltpu.make_async_copy(src.at[index], dst, local.at[1 + at])
        copy.start()
        locals_.append(copy)
    for at, (a, b) in enumerate(plane):
        to = in_plane(a, b)
        index = to[1] * 2 + to[2]
        rest.append(send(w_in.at[index], pieces[0][1], win_s.at[at], win_r.at[at], to))
        rest.append(send(w_out.at[index], pieces[1][1], wout_s.at[at], wout_r.at[at], to))
    for at, (a, b) in enumerate(column):
        to = in_column(a, b)
        index = to[0] * n_exp + to[1]
        rest.append(send(s_in.at[index], pieces[2][1], sin_s.at[at], sin_r.at[at], to))
        rest.append(send(s_out.at[index], pieces[3][1], sout_s.at[at], sout_r.at[at], to))

    for k in range(1, n_dp):
        from_z[k].wait_recv()
        spread(k, all_tok.at[rows_of(k, ex, mp)])
    from_f = {}

    def forward(kind, k, rows, to):
        at = kind * n_dp + k
        from_f[kind, k] = send(all_tok.at[rows], all_tok.at[rows], f_s.at[at], f_r.at[at], to)

    y_ex = ypeer[1]
    for k in range(n_dp):
        from_h[0, k].wait_recv()
        rows = rows_of(k, ex, 1 - mp)
        if k < n_dp // 2:
            forward(0, k, rows, ypeer)
        forward(1, k, rows, mate)
        from_h[1, k].wait_recv()
        rows = rows_of(k, y_ex, mp)
        if k >= n_dp // 2:
            forward(0, k, rows, xpeer)
        forward(2, k, rows, mate)
    for k in range(n_dp):
        from_f[0, k].wait_recv()
        forward(3, k, rows_of(k, y_ex, 1 - mp), mate)
    for k in range(n_dp):
        from_h[2, k].wait_recv()
        for kind in (1, 2, 3):
            from_f[kind, k].wait_recv()
    for copy in rest:
        copy.wait_recv()
    for copy in started:
        copy.wait_send()
    for copy in locals_:
        copy.wait()


def gather(n_dp, n_exp, tok, w_in, w_out, s_in, s_out):
    total = tok.shape[0] * n_dp * n_exp * 2
    depth = w_in.shape[1] * n_exp * 2
    n_plane, n_column = n_exp * 2 - 1, n_dp * n_exp - 1
    counts = [n_dp] * 2 + [3 * n_dp] * 2 + [4 * n_dp] * 2
    counts += [n_plane] * 4 + [n_column] * 4 + [5]
    return pl.pallas_call(
        functools.partial(gather_kernel, n_dp, n_exp),
        in_specs=[pl.BlockSpec(memory_space=pl.ANY)] * 5,
        out_specs=[pl.BlockSpec(memory_space=pl.ANY)] * 3,
        out_shape=[
            jax.ShapeDtypeStruct((total, tok.shape[1]), jnp.bfloat16),
            jax.ShapeDtypeStruct((depth, w_in.shape[2] + s_in.shape[2]), jnp.bfloat16),
            jax.ShapeDtypeStruct((depth, w_out.shape[2] + s_out.shape[2]), jnp.bfloat16),
        ],
        scratch_shapes=[pltpu.SemaphoreType.DMA((count,)) for count in counts],
        compiler_params=pltpu.CompilerParams(
            collective_id=0, has_side_effects=True, vmem_limit_bytes=VMEM_BYTES
        ),
    )(tok, w_in, w_out, s_in, s_out)


def silu(v):
    return v / (1.0 + jnp.exp(-v))


def expert_kernel(n_exp, experts, in_cols, out_cols, tok_ref, gu_ref, dn_ref, part_ref):
    dp, ex, _ = position()
    width = gu_ref.shape[0]
    mine = dp * n_exp + ex
    rows = tok_ref.shape[0]
    lane = lax.broadcasted_iota(jnp.int32, (rows, LANES), 1)
    extra = tok_ref[:, width:].astype(jnp.float32)
    weight = jnp.sum(
        jnp.where((lane == mine) | (lane == mine + experts), extra, 0.0), axis=1, keepdims=True
    )
    hid = jnp.dot(tok_ref[:, :width], gu_ref[...], preferred_element_type=jnp.float32)
    main = out_cols - LANES
    act = silu(hid[:, :main]) * hid[:, main : 2 * main] * weight
    mixed = hid[:, 2 * main : in_cols]
    mixed_act = silu(mixed) * pltpu.roll(mixed, LANES // 2, 1) * weight
    mixed_act = jnp.where(lane < LANES // 2, mixed_act, 0.0)
    span = (hid.shape[1] - in_cols) // 2
    shared = silu(hid[:, in_cols : in_cols + span]) * hid[:, in_cols + span :]
    acts = jnp.concatenate([act, mixed_act, shared], axis=1).astype(jnp.bfloat16)
    part_ref[...] = lax.dot_general(
        acts, dn_ref[...], (((1,), (1,)), ((), ())), preferred_element_type=jnp.float32
    ).astype(jnp.bfloat16)


def expert_dense(n_exp, experts, in_cols, out_cols, tok, gu, dn):
    total, wide = tok.shape
    width = gu.shape[0]
    tile = 256
    return pl.pallas_call(
        functools.partial(expert_kernel, n_exp, experts, in_cols, out_cols),
        grid=(total // tile,),
        in_specs=[
            pl.BlockSpec((tile, wide), lambda i: (i, 0)),
            pl.BlockSpec(gu.shape, lambda i: (0, 0)),
            pl.BlockSpec(dn.shape, lambda i: (0, 0)),
        ],
        out_specs=pl.BlockSpec((tile, width), lambda i: (i, 0)),
        out_shape=jax.ShapeDtypeStruct((total, width), jnp.bfloat16),
        compiler_params=pltpu.CompilerParams(vmem_limit_bytes=VMEM_BYTES),
    )(tok, gu, dn)


def scale_rows(wide, gain):
    mean_sq = jnp.mean(wide * wide, axis=-1, keepdims=True)
    return (wide * lax.rsqrt(mean_sq + 1e-06) * gain).astype(jnp.bfloat16)


def add(one, other):
    return (one.astype(jnp.float32) + other.astype(jnp.float32)).astype(jnp.bfloat16)


def reduce_kernel(
    n_dp, n_exp, part, hidden, gain, kv_w, layer, kv,
    r1, s1, r2x, r2y, s2, r3, s3, r4, rows_own, rows_peer,
    c_s, c_r, x_s, x_r, y_s, y_r, b_s, b_r, z_s, z_r, k_s, k_r,
):
    dp, ex, mp = position()
    block = hidden.shape[0]
    y, core = ex // 2, lax.rem(ex, 2)
    mate = (dp, ex + 1 - 2 * core, mp)
    xpeer = (dp, ex, 1 - mp)
    ypeer = (dp, lax.rem(ex + n_exp // 2, n_exp), mp)
    zpeers = [(lax.rem(dp + k, n_dp), ex, mp) for k in range(1, n_dp)]
    barrier([mate, xpeer, ypeer] + zpeers)
    started = []

    def send(src, dst, s, r, to):
        copy = pltpu.make_async_remote_copy(
            src_ref=src, dst_ref=dst, send_sem=s, recv_sem=r, device_id=to, device_id_type=MESH
        )
        copy.start()
        started.append(copy)
        return copy

    half = n_dp // 2
    order = [g for pair in zip(range(half), range(half, n_dp)) for g in pair]

    def pair_rows(group, c):
        index = (group // 2 * n_exp + group % 2 * 2 + c) * 2
        return pl.ds(pl.multiple_of(index * block, 2 * block), 2 * block)

    from_mate = {}
    for d in order:
        for g in (2 * d, 2 * d + 1):
            from_mate[g] = send(
                part.at[pair_rows(g, 1 - core)], r1.at[g], c_s.at[g], c_r.at[g], mate
            )
    mine = pl.ds(pl.multiple_of(mp * block, block), block)
    theirs = pl.ds(pl.multiple_of((1 - mp) * block, block), block)
    first_x, first_y = {}, {}
    for d in order:
        for g in (2 * d, 2 * d + 1):
            from_mate[g].wait_recv()
            s1[g] = add(part[pair_rows(g, core), :], r1[g])
            if d < half:
                first_x[g] = send(s1.at[g, theirs], r2x.at[g], x_s.at[g], x_r.at[g], xpeer)
        if d >= half:
            first_y[d] = send(
                s1.at[2 * d + 1 - y], r2y.at[d - half], y_s.at[d - half], y_r.at[d - half], ypeer
            )
    second = {}
    for d in order:
        if d < half:
            for j in range(2):
                g = 2 * d + j
                first_x[g].wait_recv()
                s2[d, j] = add(s1[g, mine, :], r2x[g])
            second[d] = send(s2.at[d, 1 - y], r3.at[d], b_s.at[d], b_r.at[d], ypeer)
        else:
            first_y[d].wait_recv()
            both = add(s1[2 * d + y], r2y[d - half])
            s2[d, 0] = both[:block]
            s2[d, 1] = both[block:]
            second[d] = send(s2.at[d, 1 - mp], r3.at[d], b_s.at[d], b_r.at[d], xpeer)
    for d in order:
        second[d].wait_recv()
        s3[d] = add(s2[d, y if d < half else mp], r3[d])
    third = []
    for k in range(1, n_dp):
        third.append(
            send(
                s3.at[lax.rem(dp + k, n_dp)], r4.at[k - 1], z_s.at[k - 1], z_r.at[k - 1],
                zpeers[k - 1],
            )
        )
    total = hidden[...].astype(jnp.float32) + s3[dp].astype(jnp.float32)
    for k in range(1, n_dp):
        third[k - 1].wait_recv()
        total = total + r4[k - 1].astype(jnp.float32)
    layer_rows = total.astype(jnp.bfloat16)
    layer[...] = layer_rows
    rows_own[...] = scale_rows(layer_rows.astype(jnp.float32), gain[...])
    last = send(rows_own, rows_peer, k_s.at[0], k_r.at[0], xpeer)
    kv[mine, :] = jnp.dot(
        rows_own[...], kv_w[...], preferred_element_type=jnp.float32
    ).astype(jnp.bfloat16)
    last.wait_recv()
    kv[theirs, :] = jnp.dot(
        rows_peer[...], kv_w[...], preferred_element_type=jnp.float32
    ).astype(jnp.bfloat16)
    for copy in started:
        copy.wait_send()


def reduce_tail(n_dp, n_exp, part, hidden, gain, kv_w):
    block, width = hidden.shape
    half = n_dp // 2
    bf16 = jnp.bfloat16
    shapes = [
        (2 * n_dp, 2 * block, width),
        (2 * n_dp, 2 * block, width),
        (2 * half, block, width),
        (half, 2 * block, width),
        (n_dp, 2, block, width),
        (n_dp, block, width),
        (n_dp, block, width),
        (n_dp - 1, block, width),
        (block, width),
        (block, width),
    ]
    counts = [2 * n_dp] * 2 + [2 * half] * 2 + [half] * 2 + [n_dp] * 2 + [n_dp - 1] * 2 + [1] * 2
    return pl.pallas_call(
        functools.partial(reduce_kernel, n_dp, n_exp),
        in_specs=[pl.BlockSpec(memory_space=pltpu.VMEM)] * 4,
        out_specs=[pl.BlockSpec(memory_space=pltpu.VMEM)] * 2,
        out_shape=[
            jax.ShapeDtypeStruct((block, width), bf16),
            jax.ShapeDtypeStruct((2 * block, kv_w.shape[1]), bf16),
        ],
        scratch_shapes=[pltpu.VMEM(shape, bf16) for shape in shapes]
        + [pltpu.SemaphoreType.DMA((count,)) for count in counts],
        compiler_params=pltpu.CompilerParams(
            collective_id=1, has_side_effects=True, vmem_limit_bytes=VMEM_BYTES
        ),
    )(part, hidden, gain, kv_w)


def pieces_of(weights, groups):
    rows, columns = weights.shape
    each = columns // groups
    cut = weights.reshape(rows, groups, each).transpose(1, 0, 2)
    return jnp.pad(cut, ((0, 0), (0, 0), (0, -each % LANES)))


def dense_on_device(
    hidden,
    norm_gain,
    expert_in,
    expert_out,
    expert_ids,
    gate_levels,
    shared_gate,
    shared_up,
    shared_down,
    next_gain,
    kv_weight,
):
    n_dp, n_exp = lax.axis_size("dp"), lax.axis_size("expert")
    groups = n_dp * n_exp
    experts = expert_in.shape[0] * n_dp
    w_in, w_out = pack(expert_in, expert_out)
    normed = scale_rows(hidden.astype(jnp.float32), norm_gain)
    levels = gate_levels.astype(jnp.float32)
    gate_weights = levels / jnp.sum(levels, axis=1, keepdims=True)
    chosen = expert_ids[:, :, None] == jnp.arange(experts, dtype=jnp.int32)
    spread = jnp.sum(jnp.where(chosen, gate_weights[:, :, None], 0.0), axis=1)
    high = lax.reduce_precision(spread, 8, 7)
    low = (spread - high).astype(jnp.bfloat16)
    tok = jnp.concatenate(
        [
            normed,
            high.astype(jnp.bfloat16),
            low,
            jnp.zeros((hidden.shape[0], LANES - 2 * experts), jnp.bfloat16),
        ],
        axis=1,
    )
    s_in = jnp.concatenate([pieces_of(shared_gate, groups), pieces_of(shared_up, groups)], axis=2)
    s_out = pieces_of(shared_down, groups)
    every, gu, dn = gather(n_dp, n_exp, tok, w_in, w_out, s_in, s_out)
    part = expert_dense(n_exp, experts, w_in.shape[2], w_out.shape[2], every, gu, dn)
    return tuple(reduce_tail(n_dp, n_exp, part, hidden, next_gain[None, :], kv_weight))


def dense_fits(mesh, hidden, expert_in, expert_ids):
    n_dp, n_exp, n_mp = (mesh.shape[name] for name in ("dp", "expert", "mp"))
    tokens, width = hidden.shape
    experts, _, double = expert_in.shape
    return (
        n_mp == 2
        and n_exp == 4
        and n_dp % 2 == 0
        and experts == n_dp * n_exp
        and 2 * experts <= LANES
        and double // 2 % (2 * LANES) == LANES
        and tokens * width <= 4 * 1024 * 1024
    )


def rms_scale(values, gain):
    wide = values.astype(jnp.float32)
    mean_sq = jnp.mean(wide * wide, axis=-1, keepdims=True)
    return (wide * lax.rsqrt(mean_sq + 1e-06) * gain).astype(jnp.bfloat16)


def expert_part(rows, gate_up_w, down_w):
    quarter = down_w.shape[1]
    gate_up = jnp.dot(rows, gate_up_w, preferred_element_type=jnp.float32)
    act = (jax.nn.silu(gate_up[:, :quarter]) * gate_up[:, quarter:]).astype(jnp.bfloat16)
    return lax.dot_general(
        act, down_w, (((1,), (1,)), ((), ())), preferred_element_type=jnp.float32
    )


def on_device(
    hidden,
    norm_gain,
    expert_in,
    expert_out,
    expert_ids,
    gate_levels,
    shared_gate,
    shared_up,
    shared_down,
    next_gain,
    kv_weight,
):
    tok_rows, width = hidden.shape
    top = expert_ids.shape[1]
    n_mp = lax.axis_size("mp")
    n_groups = lax.axis_size(("dp", "expert"))
    capacity = min(tok_rows, (2 * tok_rows * top + n_groups - 1) // n_groups)
    local_e, local_rows, double = expert_in.shape
    full_ff = double // 2
    quarter = full_ff // n_mp
    in_cast = (
        expert_in.astype(jnp.bfloat16)
        .reshape(local_e, local_rows, 2, n_mp, quarter)
        .transpose(0, 3, 1, 2, 4)
    )
    out_cast = (
        expert_out.astype(jnp.bfloat16)
        .reshape(local_e, local_rows, n_mp, quarter)
        .transpose(0, 2, 1, 3)
    )
    in_send = in_cast.reshape(local_e * n_mp, local_rows, 2, quarter)
    out_send = out_cast.reshape(local_e * n_mp, local_rows, quarter)
    in_recv, out_recv = (
        lax.all_to_all(in_send, ("expert", "mp"), split_axis=0, concat_axis=1, tiled=True),
        lax.all_to_all(out_send, ("expert", "mp"), split_axis=0, concat_axis=1, tiled=True),
    )
    gate_up_w = in_recv.reshape(width, 2 * quarter)
    down_w = out_recv.reshape(width, quarter)
    normed = rms_scale(hidden, norm_gain)
    levels = gate_levels.astype(jnp.float32)
    gate_weights = levels / jnp.sum(levels, axis=1, keepdims=True)
    flat_ids = expert_ids.reshape(-1)
    pairs = flat_ids.shape[0]
    onehot = (flat_ids[:, None] == jnp.arange(n_groups, dtype=jnp.int32)[None, :]).astype(jnp.int32)
    before = jnp.cumsum(onehot, axis=0) - onehot
    slot_of_pair = jnp.sum(before * onehot, axis=1)
    target = flat_ids * capacity + slot_of_pair
    token_of_pair = jnp.arange(pairs, dtype=jnp.int32) // top
    send = (
        jnp.zeros((n_groups * capacity, width), jnp.bfloat16).at[target].set(normed[token_of_pair])
    )
    received = lax.all_to_all(
        send.reshape(n_groups, capacity, width),
        ("dp", "expert"),
        split_axis=0,
        concat_axis=0,
        tiled=True,
    )
    slots_here = received.reshape(n_groups * capacity, width)
    every_slot = lax.all_gather(slots_here, "mp", axis=0, tiled=True)
    rows = every_slot
    summed = lax.psum_scatter(
        expert_part(rows, gate_up_w, down_w).astype(jnp.bfloat16),
        "mp",
        scatter_dimension=0,
        tiled=True,
    )
    result = summed.reshape(n_groups, capacity, width)
    back = lax.all_to_all(
        result, ("dp", "expert"), split_axis=0, concat_axis=0, tiled=True
    ).reshape(n_groups * capacity, width)
    picked = back[target].reshape(tok_rows, top, width)
    routed = jnp.sum(picked.astype(jnp.float32) * gate_weights[:, :, None], axis=1)
    gate_w, up_w, down_s = (
        lax.all_gather(shared_gate, ("dp", "expert"), axis=0, tiled=True),
        lax.all_gather(shared_up, ("dp", "expert"), axis=0, tiled=True),
        lax.all_gather(shared_down, ("dp", "expert"), axis=0, tiled=True),
    )
    group_rows = lax.all_gather(normed, "mp", axis=0, tiled=True)
    rows = group_rows
    gate_part = jnp.dot(rows, gate_w, preferred_element_type=jnp.float32)
    up_part = jnp.dot(rows, up_w, preferred_element_type=jnp.float32)
    act = (jax.nn.silu(gate_part) * up_part).astype(jnp.bfloat16)
    shared_out = lax.psum_scatter(
        lax.dot_general(act, down_s, (((1,), (1,)), ((), ())), preferred_element_type=jnp.float32),
        "mp",
        scatter_dimension=0,
        tiled=True,
    )
    layer_out = (hidden.astype(jnp.float32) + routed + shared_out).astype(jnp.bfloat16)
    next_rows = rms_scale(layer_out, next_gain)
    next_group = lax.all_gather(next_rows, "mp", axis=0, tiled=True)
    kv_latent = jnp.dot(next_group, kv_weight, preferred_element_type=jnp.float32).astype(
        jnp.bfloat16
    )
    return (layer_out, kv_latent)


def solution(mesh):
    in_specs = (
        P(("dp", "expert", "mp"), None),
        P(),
        P("dp", ("expert", "mp"), None),
        P("dp", ("expert", "mp"), None),
        P(("dp", "expert", "mp"), None),
        P(("dp", "expert", "mp"), None),
        P(("dp", "expert"), "mp"),
        P(("dp", "expert"), "mp"),
        P(("dp", "expert"), "mp"),
        P(),
        P(None, "mp"),
    )
    out_specs = (P(("dp", "expert", "mp"), None), P(("dp", "expert"), "mp"))

    def run(*args):
        dense = dense_fits(mesh, args[0], args[2], args[4])
        return jax.shard_map(
            dense_on_device if dense else on_device,
            mesh=mesh,
            in_specs=in_specs,
            out_specs=out_specs,
            check_vma=False,
        )(*args)

    return run
```

```python
import functools

import jax
import jax.numpy as jnp
from jax import lax
from jax.experimental import pallas as pl
from jax.experimental.pallas import tpu as pltpu
from jax.sharding import PartitionSpec as P

MESH = pl.DeviceIdType.MESH
LANES = 128
VMEM_BYTES = 56 * 1024 * 1024


def position():
    return lax.axis_index("dp"), lax.axis_index("expert"), lax.axis_index("mp")


def barrier(peers):
    sem = pltpu.get_barrier_semaphore()
    for peer in peers:
        pl.semaphore_signal(sem, inc=1, device_id=peer, device_id_type=MESH)
    pl.semaphore_wait(sem, len(peers))


def pack_kernel(in_ref, out_ref, in_pack, out_pack):
    rows, full = out_ref.shape[1:]
    main = full // (2 * LANES) * LANES
    mid = main + LANES
    half = LANES // 2
    low = lax.broadcasted_iota(jnp.int32, (rows, LANES), 1) < half
    for first, core in ((0, 0), (mid, 1)):
        in_pack[core, :, :main] = in_ref[0, :, first : first + main].astype(jnp.bfloat16)
        in_pack[core, :, main : 2 * main] = in_ref[
            0, :, full + first : full + first + main
        ].astype(jnp.bfloat16)
        out_pack[core, :, :main] = out_ref[0, :, first : first + main].astype(jnp.bfloat16)
    gate = in_ref[0, :, main:mid]
    up = in_ref[0, :, full + main : full + mid]
    down = out_ref[0, :, main:mid]
    in_pack[0, :, 2 * main :] = jnp.where(low, gate, pltpu.roll(up, half, 1)).astype(jnp.bfloat16)
    in_pack[1, :, 2 * main :] = jnp.where(low, pltpu.roll(gate, half, 1), up).astype(jnp.bfloat16)
    out_pack[0, :, main:] = jnp.where(low, down, 0.0).astype(jnp.bfloat16)
    out_pack[1, :, main:] = jnp.where(low, pltpu.roll(down, half, 1), 0.0).astype(jnp.bfloat16)


def pack(expert_in, expert_out):
    local_e, rows, double = expert_in.shape
    full = double // 2
    wide = (full // (2 * LANES) + 1) * LANES
    tile = 128
    return pl.pallas_call(
        pack_kernel,
        grid=(local_e, rows // tile),
        in_specs=[
            pl.BlockSpec((1, tile, double), lambda e, i: (e, i, 0)),
            pl.BlockSpec((1, tile, full), lambda e, i: (e, i, 0)),
        ],
        out_specs=[
            pl.BlockSpec((2, tile, full), lambda e, i: (e, i, 0)),
            pl.BlockSpec((2, tile, wide), lambda e, i: (e, i, 0)),
        ],
        out_shape=[
            jax.ShapeDtypeStruct((2 * local_e, rows, full), jnp.bfloat16),
            jax.ShapeDtypeStruct((2 * local_e, rows, wide), jnp.bfloat16),
        ],
        compiler_params=pltpu.CompilerParams(vmem_limit_bytes=VMEM_BYTES),
    )(expert_in, expert_out)


def gather_kernel(
    n_dp, n_exp, tok, w_in, w_out, s_in, s_out, all_tok, gu, dn,
    z_s, z_r, h_s, h_r, f_s, f_r, win_s, win_r, wout_s, wout_r, sin_s, sin_r, sout_s, sout_r, local,
):
    dp, ex, mp = position()
    block = tok.shape[0]
    in_cols, out_cols = w_in.shape[2], w_out.shape[2]
    w_rows, s_rows = w_in.shape[1], s_in.shape[1]
    mate = (dp, ex + 1 - 2 * lax.rem(ex, 2), mp)
    xpeer = (dp, ex, 1 - mp)
    ypeer = (dp, lax.rem(ex + n_exp // 2, n_exp), mp)
    plane = [
        (a, b) for a in range(n_exp) for b in range(2) if (a, b) != (0, 0)
    ]
    column = [
        (a, b) for a in range(n_dp) for b in range(n_exp) if (a, b) != (0, 0)
    ]

    def in_plane(a, b):
        return (dp, lax.rem(ex + a, n_exp), lax.rem(mp + b, 2))

    def in_column(a, b):
        return (lax.rem(dp + a, n_dp), lax.rem(ex + b, n_exp), mp)

    barrier(
        [in_plane(a, b) for a, b in plane] + [in_column(a, b) for a, b in column if a != 0]
    )

    def rows_of(k, e, m):
        index = (lax.rem(dp + n_dp - k, n_dp) * n_exp + e) * 2 + m
        return pl.ds(pl.multiple_of(index * block, block), block)

    started = []

    def send(src, dst, s, r, to):
        copy = pltpu.make_async_remote_copy(
            src_ref=src, dst_ref=dst, send_sem=s, recv_sem=r, device_id=to, device_id_type=MESH
        )
        copy.start()
        started.append(copy)
        return copy

    mine = rows_of(0, ex, mp)
    from_z = {}
    for k in range(1, n_dp):
        from_z[k] = send(
            tok, all_tok.at[mine], z_s.at[k], z_r.at[k], (lax.rem(dp + k, n_dp), ex, mp)
        )
    own = pltpu.make_async_copy(tok, all_tok.at[mine], local.at[0])
    own.start()
    from_h = {}

    def spread(k, src):
        rows = rows_of(k, ex, mp)
        for way, to in enumerate((xpeer, ypeer, mate)):
            at = way * n_dp + k
            from_h[way, k] = send(src, all_tok.at[rows], h_s.at[at], h_r.at[at], to)

    spread(0, tok)

    w_at = pl.ds(pl.multiple_of((ex * 2 + mp) * w_rows, w_rows), w_rows)
    s_at = pl.ds(pl.multiple_of((dp * n_exp + ex) * s_rows, s_rows), s_rows)
    rest = []
    locals_ = [own]
    pieces = (
        (w_in, gu.at[w_at, pl.ds(0, in_cols)], ex * 2 + mp),
        (w_out, dn.at[w_at, pl.ds(0, out_cols)], ex * 2 + mp),
        (s_in, gu.at[s_at, pl.ds(in_cols, s_in.shape[2])], dp * n_exp + ex),
        (s_out, dn.at[s_at, pl.ds(out_cols, s_out.shape[2])], dp * n_exp + ex),
    )
    for at, (src, dst, index) in enumerate(pieces):
        copy = pltpu.make_async_copy(src.at[index], dst, local.at[1 + at])
        copy.start()
        locals_.append(copy)
    for at, (a, b) in enumerate(plane):
        to = in_plane(a, b)
        index = to[1] * 2 + to[2]
        rest.append(send(w_in.at[index], pieces[0][1], win_s.at[at], win_r.at[at], to))
        rest.append(send(w_out.at[index], pieces[1][1], wout_s.at[at], wout_r.at[at], to))
    for at, (a, b) in enumerate(column):
        to = in_column(a, b)
        index = to[0] * n_exp + to[1]
        rest.append(send(s_in.at[index], pieces[2][1], sin_s.at[at], sin_r.at[at], to))
        rest.append(send(s_out.at[index], pieces[3][1], sout_s.at[at], sout_r.at[at], to))

    for k in range(1, n_dp):
        from_z[k].wait_recv()
        spread(k, all_tok.at[rows_of(k, ex, mp)])
    from_f = {}

    def forward(kind, k, rows, to):
        at = kind * n_dp + k
        from_f[kind, k] = send(all_tok.at[rows], all_tok.at[rows], f_s.at[at], f_r.at[at], to)

    y_ex = ypeer[1]
    for k in range(n_dp):
        from_h[0, k].wait_recv()
        rows = rows_of(k, ex, 1 - mp)
        if k < n_dp // 2:
            forward(0, k, rows, ypeer)
        forward(1, k, rows, mate)
        from_h[1, k].wait_recv()
        rows = rows_of(k, y_ex, mp)
        if k >= n_dp // 2:
            forward(0, k, rows, xpeer)
        forward(2, k, rows, mate)
    for k in range(n_dp):
        from_f[0, k].wait_recv()
        forward(3, k, rows_of(k, y_ex, 1 - mp), mate)
    for k in range(n_dp):
        from_h[2, k].wait_recv()
        for kind in (1, 2, 3):
            from_f[kind, k].wait_recv()
    for copy in rest:
        copy.wait_recv()
    for copy in started:
        copy.wait_send()
    for copy in locals_:
        copy.wait()


def gather(n_dp, n_exp, tok, w_in, w_out, s_in, s_out):
    total = tok.shape[0] * n_dp * n_exp * 2
    depth = w_in.shape[1] * n_exp * 2
    n_plane, n_column = n_exp * 2 - 1, n_dp * n_exp - 1
    counts = [n_dp] * 2 + [3 * n_dp] * 2 + [4 * n_dp] * 2
    counts += [n_plane] * 4 + [n_column] * 4 + [5]
    return pl.pallas_call(
        functools.partial(gather_kernel, n_dp, n_exp),
        in_specs=[pl.BlockSpec(memory_space=pl.ANY)] * 5,
        out_specs=[pl.BlockSpec(memory_space=pl.ANY)] * 3,
        out_shape=[
            jax.ShapeDtypeStruct((total, tok.shape[1]), jnp.bfloat16),
            jax.ShapeDtypeStruct((depth, w_in.shape[2] + s_in.shape[2]), jnp.bfloat16),
            jax.ShapeDtypeStruct((depth, w_out.shape[2] + s_out.shape[2]), jnp.bfloat16),
        ],
        scratch_shapes=[pltpu.SemaphoreType.DMA((count,)) for count in counts],
        compiler_params=pltpu.CompilerParams(
            collective_id=0, has_side_effects=True, vmem_limit_bytes=VMEM_BYTES
        ),
    )(tok, w_in, w_out, s_in, s_out)


def silu(v):
    return v / (1.0 + jnp.exp(-v))


def expert_tile(mine, experts, in_cols, out_cols, tok, gu, dn):
    width = gu.shape[0]
    rows = tok.shape[0]
    lane = lax.broadcasted_iota(jnp.int32, (rows, LANES), 1)
    extra = tok[:, width:].astype(jnp.float32)
    weight = jnp.sum(
        jnp.where((lane == mine) | (lane == mine + experts), extra, 0.0), axis=1, keepdims=True
    )
    hid = jnp.dot(tok[:, :width], gu[...], preferred_element_type=jnp.float32)
    main = out_cols - LANES
    act = silu(hid[:, :main]) * hid[:, main : 2 * main] * weight
    mixed = hid[:, 2 * main : in_cols]
    mixed_act = silu(mixed) * pltpu.roll(mixed, LANES // 2, 1) * weight
    mixed_act = jnp.where(lane < LANES // 2, mixed_act, 0.0)
    span = (hid.shape[1] - in_cols) // 2
    shared = silu(hid[:, in_cols : in_cols + span]) * hid[:, in_cols + span :]
    acts = jnp.concatenate([act, mixed_act, shared], axis=1).astype(jnp.bfloat16)
    return lax.dot_general(
        acts, dn[...], (((1,), (1,)), ((), ())), preferred_element_type=jnp.float32
    )


def scale_rows(wide, gain):
    mean_sq = jnp.mean(wide * wide, axis=-1, keepdims=True)
    return (wide * lax.rsqrt(mean_sq + 1e-06) * gain).astype(jnp.bfloat16)


def add(one, other):
    return (one.astype(jnp.float32) + other.astype(jnp.float32)).astype(jnp.bfloat16)


def expert_reduce_kernel(
    n_dp, n_exp, experts, in_cols, out_cols,
    tok_hbm, gu_hbm, dn_hbm, hidden, gain, kv_w, layer, kv,
    tok, gu, dn, pm, r1, s1, r2x, r2y, s2, r3, s3, r4, rows_own, rows_peer,
    local, c_s, c_r, x_s, x_r, y_s, y_r, b_s, b_r, z_s, z_r, k_s, k_r,
):
    dp, ex, mp = position()
    block = hidden.shape[0]
    half = n_dp // 2
    order = [d for pair in zip(range(half), range(half, n_dp)) for d in pair]
    chunk = tok.shape[1]

    loads = {}
    for at, (name, src, dst) in enumerate(
        [("gu", gu_hbm, gu), (order[0], None, None), ("dn", dn_hbm, dn)]
        + [(d, None, None) for d in order[1:]]
    ):
        if src is None:
            src, dst = tok_hbm.at[pl.ds(name * chunk, chunk)], tok.at[name]
        loads[name] = pltpu.make_async_copy(src, dst, local.at[at])
        loads[name].start()

    y, core = ex // 2, lax.rem(ex, 2)
    mate = (dp, ex + 1 - 2 * core, mp)
    xpeer = (dp, ex, 1 - mp)
    ypeer = (dp, lax.rem(ex + n_exp // 2, n_exp), mp)
    zpeers = [(lax.rem(dp + k, n_dp), ex, mp) for k in range(1, n_dp)]
    barrier([mate, xpeer, ypeer] + zpeers)
    started = []

    def remote(src, dst, s, r, to):
        return pltpu.make_async_remote_copy(
            src_ref=src, dst_ref=dst, send_sem=s, recv_sem=r, device_id=to, device_id_type=MESH
        )

    def send(src, dst, s, r, to):
        copy = remote(src, dst, s, r, to)
        copy.start()
        started.append(copy)
        return copy

    def tile(d, c):
        pairs = [
            tok[d, pl.ds(pl.multiple_of((4 * j + 2 * c) * block, 2 * block), 2 * block), :]
            for j in range(2)
        ]
        return expert_tile(
            dp * n_exp + ex, experts, in_cols, out_cols, jnp.concatenate(pairs, axis=0), gu, dn
        )

    def part_rows(j, m, count):
        return pl.ds(pl.multiple_of((2 * j + m) * block, block), count * block)

    first_x, first_y, second = {}, {}, {}

    def compute(d):
        loads[d].wait()
        pm[d] = tile(d, 1 - core).astype(jnp.bfloat16)
        from_mate = send(pm.at[d], r1.at[d], c_s.at[d], c_r.at[d], mate)
        own = tile(d, core)
        from_mate.wait_recv()
        s1[d] = (own + r1[d].astype(jnp.float32)).astype(jnp.bfloat16)
        if d < half:
            for j in range(2):
                g = 2 * d + j
                first_x[g] = send(
                    s1.at[d, part_rows(j, 1 - mp, 1)], r2x.at[g], x_s.at[g], x_r.at[g], xpeer
                )
        else:
            at = d - half
            first_y[d] = send(
                s1.at[d, part_rows(1 - y, 0, 2)], r2y.at[at], y_s.at[at], y_r.at[at], ypeer
            )

    def second_stage(d):
        if d < half:
            for j in range(2):
                g = 2 * d + j
                first_x[g].wait_recv()
                s2[d, j] = add(s1[d, part_rows(j, mp, 1), :], r2x[g])
            second[d] = send(s2.at[d, 1 - y], r3.at[d], b_s.at[d], b_r.at[d], ypeer)
        else:
            first_y[d].wait_recv()
            both = add(s1[d, part_rows(y, 0, 2), :], r2y[d - half])
            s2[d, 0] = both[:block]
            s2[d, 1] = both[block:]
            second[d] = send(s2.at[d, 1 - mp], r3.at[d], b_s.at[d], b_r.at[d], xpeer)

    def to_z(d):
        return remote(s3.at[d], r4.at[dp], z_s.at[d], z_r.at[dp], (d, ex, mp))

    def third_stage(d):
        second[d].wait_recv()
        s3[d] = add(s2[d, y if d < half else mp], r3[d])

        @pl.when(dp != d)
        def _():
            to_z(d).start()

    loads["gu"].wait()
    loads["dn"].wait()
    lag = 2
    for at, d in enumerate(order):
        compute(d)
        if at >= lag:
            second_stage(order[at - lag])
    for at in range(max(0, n_dp - lag), n_dp):
        second_stage(order[at])
        third_stage(order[at - n_dp + lag])
    for at in range(lag, n_dp):
        third_stage(order[at])

    total = hidden[...].astype(jnp.float32) + s3[dp].astype(jnp.float32)
    for k in range(1, n_dp):
        other = lax.rem(dp + k, n_dp)
        remote(s3.at[other], r4.at[other], z_s.at[other], z_r.at[other], zpeers[k - 1]).wait_recv()
        total = total + r4[other].astype(jnp.float32)
    layer_rows = total.astype(jnp.bfloat16)
    layer[...] = layer_rows
    rows_own[...] = scale_rows(layer_rows.astype(jnp.float32), gain[...])
    last = send(rows_own, rows_peer, k_s.at[0], k_r.at[0], xpeer)
    mine = pl.ds(pl.multiple_of(mp * block, block), block)
    theirs = pl.ds(pl.multiple_of((1 - mp) * block, block), block)
    kv[mine, :] = jnp.dot(
        rows_own[...], kv_w[...], preferred_element_type=jnp.float32
    ).astype(jnp.bfloat16)
    last.wait_recv()
    kv[theirs, :] = jnp.dot(
        rows_peer[...], kv_w[...], preferred_element_type=jnp.float32
    ).astype(jnp.bfloat16)
    for copy in started:
        copy.wait_send()
    for d in range(n_dp):

        @pl.when(dp != d)
        def _(d=d):
            to_z(d).wait_send()


def expert_reduce(n_dp, n_exp, experts, in_cols, out_cols, tok, gu, dn, hidden, gain, kv_w):
    block, width = hidden.shape
    half = n_dp // 2
    bf16 = jnp.bfloat16
    shapes = [
        (n_dp, tok.shape[0] // n_dp, tok.shape[1]),
        gu.shape,
        dn.shape,
        (n_dp, 4 * block, width),
        (n_dp, 4 * block, width),
        (n_dp, 4 * block, width),
        (2 * half, block, width),
        (half, 2 * block, width),
        (n_dp, 2, block, width),
        (n_dp, block, width),
        (n_dp, block, width),
        (n_dp, block, width),
        (block, width),
        (block, width),
    ]
    counts = [n_dp + 2] + [n_dp] * 2 + [2 * half] * 2 + [half] * 2 + [n_dp] * 4 + [1] * 2
    return pl.pallas_call(
        functools.partial(expert_reduce_kernel, n_dp, n_exp, experts, in_cols, out_cols),
        in_specs=[pl.BlockSpec(memory_space=pl.ANY)] * 3
        + [pl.BlockSpec(memory_space=pltpu.VMEM)] * 3,
        out_specs=[pl.BlockSpec(memory_space=pltpu.VMEM)] * 2,
        out_shape=[
            jax.ShapeDtypeStruct((block, width), bf16),
            jax.ShapeDtypeStruct((2 * block, kv_w.shape[1]), bf16),
        ],
        scratch_shapes=[pltpu.VMEM(shape, bf16) for shape in shapes]
        + [pltpu.SemaphoreType.DMA((count,)) for count in counts],
        compiler_params=pltpu.CompilerParams(
            collective_id=1, has_side_effects=True, vmem_limit_bytes=VMEM_BYTES
        ),
    )(tok, gu, dn, hidden, gain, kv_w)


def pieces_of(weights, groups):
    rows, columns = weights.shape
    each = columns // groups
    cut = weights.reshape(rows, groups, each).transpose(1, 0, 2)
    return jnp.pad(cut, ((0, 0), (0, 0), (0, -each % LANES)))


def dense_on_device(
    hidden,
    norm_gain,
    expert_in,
    expert_out,
    expert_ids,
    gate_levels,
    shared_gate,
    shared_up,
    shared_down,
    next_gain,
    kv_weight,
):
    n_dp, n_exp = lax.axis_size("dp"), lax.axis_size("expert")
    groups = n_dp * n_exp
    experts = expert_in.shape[0] * n_dp
    w_in, w_out = pack(expert_in, expert_out)
    normed = scale_rows(hidden.astype(jnp.float32), norm_gain)
    levels = gate_levels.astype(jnp.float32)
    gate_weights = levels / jnp.sum(levels, axis=1, keepdims=True)
    chosen = expert_ids[:, :, None] == jnp.arange(experts, dtype=jnp.int32)
    spread = jnp.sum(jnp.where(chosen, gate_weights[:, :, None], 0.0), axis=1)
    high = lax.reduce_precision(spread, 8, 7)
    low = (spread - high).astype(jnp.bfloat16)
    tok = jnp.concatenate(
        [
            normed,
            high.astype(jnp.bfloat16),
            low,
            jnp.zeros((hidden.shape[0], LANES - 2 * experts), jnp.bfloat16),
        ],
        axis=1,
    )
    s_in = jnp.concatenate([pieces_of(shared_gate, groups), pieces_of(shared_up, groups)], axis=2)
    s_out = pieces_of(shared_down, groups)
    every, gu, dn = gather(n_dp, n_exp, tok, w_in, w_out, s_in, s_out)
    return tuple(
        expert_reduce(
            n_dp, n_exp, experts, w_in.shape[2], w_out.shape[2],
            every, gu, dn, hidden, next_gain[None, :], kv_weight,
        )
    )


def dense_fits(mesh, hidden, expert_in, expert_ids):
    n_dp, n_exp, n_mp = (mesh.shape[name] for name in ("dp", "expert", "mp"))
    tokens, width = hidden.shape
    experts, _, double = expert_in.shape
    return (
        n_mp == 2
        and n_exp == 4
        and n_dp % 2 == 0
        and experts == n_dp * n_exp
        and 2 * experts <= LANES
        and double // 2 % (2 * LANES) == LANES
        and tokens * width <= 4 * 1024 * 1024
    )


def rms_scale(values, gain):
    wide = values.astype(jnp.float32)
    mean_sq = jnp.mean(wide * wide, axis=-1, keepdims=True)
    return (wide * lax.rsqrt(mean_sq + 1e-06) * gain).astype(jnp.bfloat16)


def expert_part(rows, gate_up_w, down_w):
    quarter = down_w.shape[1]
    gate_up = jnp.dot(rows, gate_up_w, preferred_element_type=jnp.float32)
    act = (jax.nn.silu(gate_up[:, :quarter]) * gate_up[:, quarter:]).astype(jnp.bfloat16)
    return lax.dot_general(
        act, down_w, (((1,), (1,)), ((), ())), preferred_element_type=jnp.float32
    )


def on_device(
    hidden,
    norm_gain,
    expert_in,
    expert_out,
    expert_ids,
    gate_levels,
    shared_gate,
    shared_up,
    shared_down,
    next_gain,
    kv_weight,
):
    tok_rows, width = hidden.shape
    top = expert_ids.shape[1]
    n_mp = lax.axis_size("mp")
    n_groups = lax.axis_size(("dp", "expert"))
    capacity = min(tok_rows, (2 * tok_rows * top + n_groups - 1) // n_groups)
    local_e, local_rows, double = expert_in.shape
    full_ff = double // 2
    quarter = full_ff // n_mp
    in_cast = (
        expert_in.astype(jnp.bfloat16)
        .reshape(local_e, local_rows, 2, n_mp, quarter)
        .transpose(0, 3, 1, 2, 4)
    )
    out_cast = (
        expert_out.astype(jnp.bfloat16)
        .reshape(local_e, local_rows, n_mp, quarter)
        .transpose(0, 2, 1, 3)
    )
    in_send = in_cast.reshape(local_e * n_mp, local_rows, 2, quarter)
    out_send = out_cast.reshape(local_e * n_mp, local_rows, quarter)
    in_recv, out_recv = (
        lax.all_to_all(in_send, ("expert", "mp"), split_axis=0, concat_axis=1, tiled=True),
        lax.all_to_all(out_send, ("expert", "mp"), split_axis=0, concat_axis=1, tiled=True),
    )
    gate_up_w = in_recv.reshape(width, 2 * quarter)
    down_w = out_recv.reshape(width, quarter)
    normed = rms_scale(hidden, norm_gain)
    levels = gate_levels.astype(jnp.float32)
    gate_weights = levels / jnp.sum(levels, axis=1, keepdims=True)
    flat_ids = expert_ids.reshape(-1)
    pairs = flat_ids.shape[0]
    onehot = (flat_ids[:, None] == jnp.arange(n_groups, dtype=jnp.int32)[None, :]).astype(jnp.int32)
    before = jnp.cumsum(onehot, axis=0) - onehot
    slot_of_pair = jnp.sum(before * onehot, axis=1)
    target = flat_ids * capacity + slot_of_pair
    token_of_pair = jnp.arange(pairs, dtype=jnp.int32) // top
    send = (
        jnp.zeros((n_groups * capacity, width), jnp.bfloat16).at[target].set(normed[token_of_pair])
    )
    received = lax.all_to_all(
        send.reshape(n_groups, capacity, width),
        ("dp", "expert"),
        split_axis=0,
        concat_axis=0,
        tiled=True,
    )
    slots_here = received.reshape(n_groups * capacity, width)
    every_slot = lax.all_gather(slots_here, "mp", axis=0, tiled=True)
    rows = every_slot
    summed = lax.psum_scatter(
        expert_part(rows, gate_up_w, down_w).astype(jnp.bfloat16),
        "mp",
        scatter_dimension=0,
        tiled=True,
    )
    result = summed.reshape(n_groups, capacity, width)
    back = lax.all_to_all(
        result, ("dp", "expert"), split_axis=0, concat_axis=0, tiled=True
    ).reshape(n_groups * capacity, width)
    picked = back[target].reshape(tok_rows, top, width)
    routed = jnp.sum(picked.astype(jnp.float32) * gate_weights[:, :, None], axis=1)
    gate_w, up_w, down_s = (
        lax.all_gather(shared_gate, ("dp", "expert"), axis=0, tiled=True),
        lax.all_gather(shared_up, ("dp", "expert"), axis=0, tiled=True),
        lax.all_gather(shared_down, ("dp", "expert"), axis=0, tiled=True),
    )
    group_rows = lax.all_gather(normed, "mp", axis=0, tiled=True)
    rows = group_rows
    gate_part = jnp.dot(rows, gate_w, preferred_element_type=jnp.float32)
    up_part = jnp.dot(rows, up_w, preferred_element_type=jnp.float32)
    act = (jax.nn.silu(gate_part) * up_part).astype(jnp.bfloat16)
    shared_out = lax.psum_scatter(
        lax.dot_general(act, down_s, (((1,), (1,)), ((), ())), preferred_element_type=jnp.float32),
        "mp",
        scatter_dimension=0,
        tiled=True,
    )
    layer_out = (hidden.astype(jnp.float32) + routed + shared_out).astype(jnp.bfloat16)
    next_rows = rms_scale(layer_out, next_gain)
    next_group = lax.all_gather(next_rows, "mp", axis=0, tiled=True)
    kv_latent = jnp.dot(next_group, kv_weight, preferred_element_type=jnp.float32).astype(
        jnp.bfloat16
    )
    return (layer_out, kv_latent)


def solution(mesh):
    in_specs = (
        P(("dp", "expert", "mp"), None),
        P(),
        P("dp", ("expert", "mp"), None),
        P("dp", ("expert", "mp"), None),
        P(("dp", "expert", "mp"), None),
        P(("dp", "expert", "mp"), None),
        P(("dp", "expert"), "mp"),
        P(("dp", "expert"), "mp"),
        P(("dp", "expert"), "mp"),
        P(),
        P(None, "mp"),
    )
    out_specs = (P(("dp", "expert", "mp"), None), P(("dp", "expert"), "mp"))

    def run(*args):
        dense = dense_fits(mesh, args[0], args[2], args[4])
        return jax.shard_map(
            dense_on_device if dense else on_device,
            mesh=mesh,
            in_specs=in_specs,
            out_specs=out_specs,
            check_vma=False,
        )(*args)

    return run
```

```python
import functools

import jax
import jax.numpy as jnp
from jax import lax
from jax.experimental import pallas as pl
from jax.experimental.pallas import tpu as pltpu
from jax.sharding import PartitionSpec as P

MESH = pl.DeviceIdType.MESH
LANES = 128
VMEM_BYTES = 56 * 1024 * 1024


def position():
    return lax.axis_index("dp"), lax.axis_index("expert"), lax.axis_index("mp")


def barrier(peers):
    sem = pltpu.get_barrier_semaphore()
    for peer in peers:
        pl.semaphore_signal(sem, inc=1, device_id=peer, device_id_type=MESH)
    pl.semaphore_wait(sem, len(peers))


def pack_piece(e, wide_in, wide_out, in_pack, out_pack):
    rows, full = wide_out.shape[1:]
    main = full // (2 * LANES) * LANES
    mid = main + LANES
    half = LANES // 2
    low = lax.broadcasted_iota(jnp.int32, (rows, LANES), 1) < half
    bf16 = jnp.bfloat16
    for first, side in ((0, 0), (mid, 1)):
        in_pack[e, side, :, :main] = wide_in[e, :, first : first + main].astype(bf16)
        in_pack[e, side, :, main : 2 * main] = wide_in[
            e, :, full + first : full + first + main
        ].astype(bf16)
        out_pack[e, side, :, :main] = wide_out[e, :, first : first + main].astype(bf16)
    gate = wide_in[e, :, main:mid]
    up = wide_in[e, :, full + main : full + mid]
    down = wide_out[e, :, main:mid]
    in_pack[e, 0, :, 2 * main :] = jnp.where(low, gate, pltpu.roll(up, half, 1)).astype(bf16)
    in_pack[e, 1, :, 2 * main :] = jnp.where(low, pltpu.roll(gate, half, 1), up).astype(bf16)
    out_pack[e, 0, :, main:] = jnp.where(low, down, 0.0).astype(bf16)
    out_pack[e, 1, :, main:] = jnp.where(low, pltpu.roll(down, half, 1), 0.0).astype(bf16)


def gather_kernel(
    n_dp, n_exp, tok, expert_in, expert_out, s_in, s_out, all_tok, gu, dn,
    wide_in, wide_out, w_in, w_out,
    z_s, z_r, h_s, h_r, f_s, f_r, win_s, win_r, wout_s, wout_r, sin_s, sin_r, sout_s, sout_r, local,
):
    dp, ex, mp = position()
    block = tok.shape[0]
    in_cols, out_cols = w_in.shape[3], w_out.shape[3]
    w_rows, s_rows = w_in.shape[2], s_in.shape[1]
    mate = (dp, ex + 1 - 2 * lax.rem(ex, 2), mp)
    xpeer = (dp, ex, 1 - mp)
    ypeer = (dp, lax.rem(ex + n_exp // 2, n_exp), mp)
    plane = [
        (a, b) for a in range(n_exp) for b in range(2) if (a, b) != (0, 0)
    ]
    column = [
        (a, b) for a in range(n_dp) for b in range(n_exp) if (a, b) != (0, 0)
    ]

    def in_plane(a, b):
        return (dp, lax.rem(ex + a, n_exp), lax.rem(mp + b, 2))

    def in_column(a, b):
        return (lax.rem(dp + a, n_dp), lax.rem(ex + b, n_exp), mp)

    y_ex = ypeer[1]
    targets = [y_ex, ex, lax.rem(mate[1] + n_exp // 2, n_exp), mate[1]]
    loads = []
    for kind, e in enumerate(targets):
        for src, dst, at in ((expert_in, wide_in, 3), (expert_out, wide_out, 4)):
            copy = pltpu.make_async_copy(src.at[e], dst.at[e], local.at[at + 2 * kind])
            copy.start()
            loads.append(copy)

    barrier(
        [in_plane(a, b) for a, b in plane] + [in_column(a, b) for a, b in column if a != 0]
    )

    def rows_of(k, e, m):
        index = (lax.rem(dp + n_dp - k, n_dp) * n_exp + e) * 2 + m
        return pl.ds(pl.multiple_of(index * block, block), block)

    started = []

    def send(src, dst, s, r, to):
        copy = pltpu.make_async_remote_copy(
            src_ref=src, dst_ref=dst, send_sem=s, recv_sem=r, device_id=to, device_id_type=MESH
        )
        copy.start()
        started.append(copy)
        return copy

    mine = rows_of(0, ex, mp)
    from_z = {}
    for k in range(1, n_dp):
        from_z[k] = send(
            tok, all_tok.at[mine], z_s.at[k], z_r.at[k], (lax.rem(dp + k, n_dp), ex, mp)
        )
    own = pltpu.make_async_copy(tok, all_tok.at[mine], local.at[0])
    own.start()
    from_h = {}

    def spread(k, src):
        rows = rows_of(k, ex, mp)
        for way, to in enumerate((xpeer, ypeer, mate)):
            at = way * n_dp + k
            from_h[way, k] = send(src, all_tok.at[rows], h_s.at[at], h_r.at[at], to)

    spread(0, tok)

    w_at = pl.ds(pl.multiple_of((ex * 2 + mp) * w_rows, w_rows), w_rows)
    s_at = pl.ds(pl.multiple_of((dp * n_exp + ex) * s_rows, s_rows), s_rows)
    rest = []
    locals_ = [own]
    gu_at, dn_at = gu.at[w_at, pl.ds(0, in_cols)], dn.at[w_at, pl.ds(0, out_cols)]
    gu_s = gu.at[s_at, pl.ds(in_cols, s_in.shape[2])]
    dn_s = dn.at[s_at, pl.ds(out_cols, s_out.shape[2])]

    def keep(src, dst, at):
        copy = pltpu.make_async_copy(src, dst, local.at[at])
        copy.start()
        locals_.append(copy)

    def weights(kind):
        e = targets[kind]
        loads[2 * kind].wait()
        loads[2 * kind + 1].wait()
        pack_piece(e, wide_in, wide_out, w_in, w_out)
        for b in range(2):
            m = lax.rem(mp + b, 2)
            at = 2 * kind + b
            if kind == 1 and b == 0:
                keep(w_in.at[e, m], gu_at, 3 + 2 * n_exp)
                keep(w_out.at[e, m], dn_at, 4 + 2 * n_exp)
                continue
            to = (dp, e, m)
            rest.append(send(w_in.at[e, m], gu_at, win_s.at[at], win_r.at[at], to))
            rest.append(send(w_out.at[e, m], dn_at, wout_s.at[at], wout_r.at[at], to))

    weights(0)
    keep(s_in.at[dp * n_exp + ex], gu_s, 1)
    keep(s_out.at[dp * n_exp + ex], dn_s, 2)
    for at, (a, b) in enumerate(column):
        to = in_column(a, b)
        index = to[0] * n_exp + to[1]
        rest.append(send(s_in.at[index], gu_s, sin_s.at[at], sin_r.at[at], to))
        rest.append(send(s_out.at[index], dn_s, sout_s.at[at], sout_r.at[at], to))
    weights(1)

    for k in range(1, n_dp):
        from_z[k].wait_recv()
        spread(k, all_tok.at[rows_of(k, ex, mp)])
    weights(2)
    weights(3)
    from_f = {}

    def forward(kind, k, rows, to):
        at = kind * n_dp + k
        from_f[kind, k] = send(all_tok.at[rows], all_tok.at[rows], f_s.at[at], f_r.at[at], to)

    over_y = n_dp // 4
    for k in range(n_dp):
        from_h[0, k].wait_recv()
        rows = rows_of(k, ex, 1 - mp)
        if k < over_y:
            forward(0, k, rows, ypeer)
        forward(1, k, rows, mate)
        from_h[1, k].wait_recv()
        rows = rows_of(k, y_ex, mp)
        if k >= over_y:
            forward(0, k, rows, xpeer)
        forward(2, k, rows, mate)
    for k in range(n_dp):
        from_f[0, k].wait_recv()
        forward(3, k, rows_of(k, y_ex, 1 - mp), mate)
    for k in range(n_dp):
        from_h[2, k].wait_recv()
        for kind in (1, 2, 3):
            from_f[kind, k].wait_recv()
    for copy in rest:
        copy.wait_recv()
    for copy in started:
        copy.wait_send()
    for copy in locals_:
        copy.wait()


def gather(n_dp, n_exp, tok, expert_in, expert_out, s_in, s_out):
    total = tok.shape[0] * n_dp * n_exp * 2
    local_e, rows, full = expert_out.shape
    depth = rows * n_exp * 2
    wide = (full // (2 * LANES) + 1) * LANES
    n_plane, n_column = n_exp * 2, n_dp * n_exp - 1
    counts = [n_dp] * 2 + [3 * n_dp] * 2 + [4 * n_dp] * 2
    counts += [n_plane] * 4 + [n_column] * 4 + [5 + 2 * n_exp]
    bf16 = jnp.bfloat16
    return pl.pallas_call(
        functools.partial(gather_kernel, n_dp, n_exp),
        in_specs=[pl.BlockSpec(memory_space=pl.ANY)] * 5,
        out_specs=[pl.BlockSpec(memory_space=pl.ANY)] * 3,
        out_shape=[
            jax.ShapeDtypeStruct((total, tok.shape[1]), bf16),
            jax.ShapeDtypeStruct((depth, full + s_in.shape[2]), bf16),
            jax.ShapeDtypeStruct((depth, wide + s_out.shape[2]), bf16),
        ],
        scratch_shapes=[
            pltpu.VMEM(expert_in.shape, jnp.float32),
            pltpu.VMEM(expert_out.shape, jnp.float32),
            pltpu.VMEM((local_e, 2, rows, full), bf16),
            pltpu.VMEM((local_e, 2, rows, wide), bf16),
        ]
        + [pltpu.SemaphoreType.DMA((count,)) for count in counts],
        compiler_params=pltpu.CompilerParams(
            collective_id=0, has_side_effects=True, vmem_limit_bytes=VMEM_BYTES
        ),
    )(tok, expert_in, expert_out, s_in, s_out)


def silu(v):
    return v / (1.0 + jnp.exp(-v))


def expert_tile(mine, experts, in_cols, out_cols, tok, gu, dn):
    width = gu.shape[0]
    rows = tok.shape[0]
    lane = lax.broadcasted_iota(jnp.int32, (rows, LANES), 1)
    extra = tok[:, width:].astype(jnp.float32)
    weight = jnp.sum(
        jnp.where((lane == mine) | (lane == mine + experts), extra, 0.0), axis=1, keepdims=True
    )
    hid = jnp.dot(tok[:, :width], gu[...], preferred_element_type=jnp.float32)
    main = out_cols - LANES
    act = silu(hid[:, :main]) * hid[:, main : 2 * main] * weight
    mixed = hid[:, 2 * main : in_cols]
    mixed_act = silu(mixed) * pltpu.roll(mixed, LANES // 2, 1) * weight
    mixed_act = jnp.where(lane < LANES // 2, mixed_act, 0.0)
    span = (hid.shape[1] - in_cols) // 2
    shared = silu(hid[:, in_cols : in_cols + span]) * hid[:, in_cols + span :]
    acts = jnp.concatenate([act, mixed_act, shared], axis=1).astype(jnp.bfloat16)
    return lax.dot_general(
        acts, dn[...], (((1,), (1,)), ((), ())), preferred_element_type=jnp.float32
    )


def scale_rows(wide, gain):
    mean_sq = jnp.mean(wide * wide, axis=-1, keepdims=True)
    return (wide * lax.rsqrt(mean_sq + 1e-06) * gain).astype(jnp.bfloat16)


def add(one, other):
    return (one.astype(jnp.float32) + other.astype(jnp.float32)).astype(jnp.bfloat16)


def expert_reduce_kernel(
    n_dp, n_exp, experts, in_cols, out_cols,
    tok_hbm, gu_hbm, dn_hbm, hidden, gain, kv_w, layer, kv,
    tok, gu, dn, pm, r1, s1, r2x, r2y, s2, r3, s3, r4, rows_own, rows_peer,
    local, c_s, c_r, x_s, x_r, y_s, y_r, b_s, b_r, z_s, z_r, k_s, k_r,
):
    dp, ex, mp = position()
    block = hidden.shape[0]
    half = n_dp // 2
    order = [d for pair in zip(range(half), range(half, n_dp)) for d in pair]
    chunk = tok.shape[1]

    loads = {}
    for at, (name, src, dst) in enumerate(
        [("gu", gu_hbm, gu), (order[0], None, None), ("dn", dn_hbm, dn)]
        + [(d, None, None) for d in order[1:]]
    ):
        if src is None:
            src, dst = tok_hbm.at[pl.ds(name * chunk, chunk)], tok.at[name]
        loads[name] = pltpu.make_async_copy(src, dst, local.at[at])
        loads[name].start()

    y, core = ex // 2, lax.rem(ex, 2)
    mate = (dp, ex + 1 - 2 * core, mp)
    xpeer = (dp, ex, 1 - mp)
    ypeer = (dp, lax.rem(ex + n_exp // 2, n_exp), mp)
    zpeers = [(lax.rem(dp + k, n_dp), ex, mp) for k in range(1, n_dp)]
    barrier([mate, xpeer, ypeer] + zpeers)
    started = []

    def remote(src, dst, s, r, to):
        return pltpu.make_async_remote_copy(
            src_ref=src, dst_ref=dst, send_sem=s, recv_sem=r, device_id=to, device_id_type=MESH
        )

    def send(src, dst, s, r, to):
        copy = remote(src, dst, s, r, to)
        copy.start()
        started.append(copy)
        return copy

    def tile(d, c):
        pairs = [
            tok[d, pl.ds(pl.multiple_of((4 * j + 2 * c) * block, 2 * block), 2 * block), :]
            for j in range(2)
        ]
        return expert_tile(
            dp * n_exp + ex, experts, in_cols, out_cols, jnp.concatenate(pairs, axis=0), gu, dn
        )

    def part_rows(j, m, count):
        return pl.ds(pl.multiple_of((2 * j + m) * block, block), count * block)

    first_x, first_y, second = {}, {}, {}

    def compute(d):
        loads[d].wait()
        pm[d] = tile(d, 1 - core).astype(jnp.bfloat16)
        from_mate = send(pm.at[d], r1.at[d], c_s.at[d], c_r.at[d], mate)
        own = tile(d, core)
        from_mate.wait_recv()
        s1[d] = (own + r1[d].astype(jnp.float32)).astype(jnp.bfloat16)
        if d < half:
            for j in range(2):
                g = 2 * d + j
                first_x[g] = send(
                    s1.at[d, part_rows(j, 1 - mp, 1)], r2x.at[g], x_s.at[g], x_r.at[g], xpeer
                )
        else:
            at = d - half
            first_y[d] = send(
                s1.at[d, part_rows(1 - y, 0, 2)], r2y.at[at], y_s.at[at], y_r.at[at], ypeer
            )

    def second_stage(d):
        if d < half:
            for j in range(2):
                g = 2 * d + j
                first_x[g].wait_recv()
                s2[d, j] = add(s1[d, part_rows(j, mp, 1), :], r2x[g])
            second[d] = send(s2.at[d, 1 - y], r3.at[d], b_s.at[d], b_r.at[d], ypeer)
        else:
            first_y[d].wait_recv()
            both = add(s1[d, part_rows(y, 0, 2), :], r2y[d - half])
            s2[d, 0] = both[:block]
            s2[d, 1] = both[block:]
            second[d] = send(s2.at[d, 1 - mp], r3.at[d], b_s.at[d], b_r.at[d], xpeer)

    def to_z(d):
        return remote(s3.at[d], r4.at[dp], z_s.at[d], z_r.at[dp], (d, ex, mp))

    def third_stage(d):
        second[d].wait_recv()
        s3[d] = add(s2[d, y if d < half else mp], r3[d])

        @pl.when(dp != d)
        def _():
            to_z(d).start()

    loads["gu"].wait()
    loads["dn"].wait()
    lag = 2
    for at, d in enumerate(order):
        compute(d)
        if at >= lag:
            second_stage(order[at - lag])
    for at in range(max(0, n_dp - lag), n_dp):
        second_stage(order[at])
        third_stage(order[at - n_dp + lag])
    for at in range(lag, n_dp):
        third_stage(order[at])

    total = hidden[...].astype(jnp.float32) + s3[dp].astype(jnp.float32)
    for k in range(1, n_dp):
        other = lax.rem(dp + k, n_dp)
        remote(s3.at[other], r4.at[other], z_s.at[other], z_r.at[other], zpeers[k - 1]).wait_recv()
        total = total + r4[other].astype(jnp.float32)
    layer_rows = total.astype(jnp.bfloat16)
    layer[...] = layer_rows
    rows_own[...] = scale_rows(layer_rows.astype(jnp.float32), gain[...])
    last = send(rows_own, rows_peer, k_s.at[0], k_r.at[0], xpeer)
    mine = pl.ds(pl.multiple_of(mp * block, block), block)
    theirs = pl.ds(pl.multiple_of((1 - mp) * block, block), block)
    kv[mine, :] = jnp.dot(
        rows_own[...], kv_w[...], preferred_element_type=jnp.float32
    ).astype(jnp.bfloat16)
    last.wait_recv()
    kv[theirs, :] = jnp.dot(
        rows_peer[...], kv_w[...], preferred_element_type=jnp.float32
    ).astype(jnp.bfloat16)
    for copy in started:
        copy.wait_send()
    for d in range(n_dp):

        @pl.when(dp != d)
        def _(d=d):
            to_z(d).wait_send()


def expert_reduce(n_dp, n_exp, experts, in_cols, out_cols, tok, gu, dn, hidden, gain, kv_w):
    block, width = hidden.shape
    half = n_dp // 2
    bf16 = jnp.bfloat16
    shapes = [
        (n_dp, tok.shape[0] // n_dp, tok.shape[1]),
        gu.shape,
        dn.shape,
        (n_dp, 4 * block, width),
        (n_dp, 4 * block, width),
        (n_dp, 4 * block, width),
        (2 * half, block, width),
        (half, 2 * block, width),
        (n_dp, 2, block, width),
        (n_dp, block, width),
        (n_dp, block, width),
        (n_dp, block, width),
        (block, width),
        (block, width),
    ]
    counts = [n_dp + 2] + [n_dp] * 2 + [2 * half] * 2 + [half] * 2 + [n_dp] * 4 + [1] * 2
    return pl.pallas_call(
        functools.partial(expert_reduce_kernel, n_dp, n_exp, experts, in_cols, out_cols),
        in_specs=[pl.BlockSpec(memory_space=pl.ANY)] * 3
        + [pl.BlockSpec(memory_space=pltpu.VMEM)] * 3,
        out_specs=[pl.BlockSpec(memory_space=pltpu.VMEM)] * 2,
        out_shape=[
            jax.ShapeDtypeStruct((block, width), bf16),
            jax.ShapeDtypeStruct((2 * block, kv_w.shape[1]), bf16),
        ],
        scratch_shapes=[pltpu.VMEM(shape, bf16) for shape in shapes]
        + [pltpu.SemaphoreType.DMA((count,)) for count in counts],
        compiler_params=pltpu.CompilerParams(
            collective_id=1, has_side_effects=True, vmem_limit_bytes=VMEM_BYTES
        ),
    )(tok, gu, dn, hidden, gain, kv_w)


def pieces_of(weights, groups):
    rows, columns = weights.shape
    each = columns // groups
    cut = weights.reshape(rows, groups, each).transpose(1, 0, 2)
    return jnp.pad(cut, ((0, 0), (0, 0), (0, -each % LANES)))


def dense_on_device(
    hidden,
    norm_gain,
    expert_in,
    expert_out,
    expert_ids,
    gate_levels,
    shared_gate,
    shared_up,
    shared_down,
    next_gain,
    kv_weight,
):
    n_dp, n_exp = lax.axis_size("dp"), lax.axis_size("expert")
    groups = n_dp * n_exp
    experts = expert_in.shape[0] * n_dp
    normed = scale_rows(hidden.astype(jnp.float32), norm_gain)
    levels = gate_levels.astype(jnp.float32)
    gate_weights = levels / jnp.sum(levels, axis=1, keepdims=True)
    chosen = expert_ids[:, :, None] == jnp.arange(experts, dtype=jnp.int32)
    spread = jnp.sum(jnp.where(chosen, gate_weights[:, :, None], 0.0), axis=1)
    high = lax.reduce_precision(spread, 8, 7)
    low = (spread - high).astype(jnp.bfloat16)
    tok = jnp.concatenate(
        [
            normed,
            high.astype(jnp.bfloat16),
            low,
            jnp.zeros((hidden.shape[0], LANES - 2 * experts), jnp.bfloat16),
        ],
        axis=1,
    )
    s_in = jnp.concatenate([pieces_of(shared_gate, groups), pieces_of(shared_up, groups)], axis=2)
    s_out = pieces_of(shared_down, groups)
    every, gu, dn = gather(n_dp, n_exp, tok, expert_in, expert_out, s_in, s_out)
    in_cols, out_cols = gu.shape[1] - s_in.shape[2], dn.shape[1] - s_out.shape[2]
    return tuple(
        expert_reduce(
            n_dp, n_exp, experts, in_cols, out_cols,
            every, gu, dn, hidden, next_gain[None, :], kv_weight,
        )
    )


def dense_fits(mesh, hidden, expert_in, expert_ids):
    n_dp, n_exp, n_mp = (mesh.shape[name] for name in ("dp", "expert", "mp"))
    tokens, width = hidden.shape
    experts, _, double = expert_in.shape
    return (
        n_mp == 2
        and n_exp == 4
        and n_dp % 2 == 0
        and experts == n_dp * n_exp
        and 2 * experts <= LANES
        and double // 2 % (2 * LANES) == LANES
        and tokens * width <= 4 * 1024 * 1024
    )


def rms_scale(values, gain):
    wide = values.astype(jnp.float32)
    mean_sq = jnp.mean(wide * wide, axis=-1, keepdims=True)
    return (wide * lax.rsqrt(mean_sq + 1e-06) * gain).astype(jnp.bfloat16)


def expert_part(rows, gate_up_w, down_w):
    quarter = down_w.shape[1]
    gate_up = jnp.dot(rows, gate_up_w, preferred_element_type=jnp.float32)
    act = (jax.nn.silu(gate_up[:, :quarter]) * gate_up[:, quarter:]).astype(jnp.bfloat16)
    return lax.dot_general(
        act, down_w, (((1,), (1,)), ((), ())), preferred_element_type=jnp.float32
    )


def on_device(
    hidden,
    norm_gain,
    expert_in,
    expert_out,
    expert_ids,
    gate_levels,
    shared_gate,
    shared_up,
    shared_down,
    next_gain,
    kv_weight,
):
    tok_rows, width = hidden.shape
    top = expert_ids.shape[1]
    n_mp = lax.axis_size("mp")
    n_groups = lax.axis_size(("dp", "expert"))
    capacity = min(tok_rows, (2 * tok_rows * top + n_groups - 1) // n_groups)
    local_e, local_rows, double = expert_in.shape
    full_ff = double // 2
    quarter = full_ff // n_mp
    in_cast = (
        expert_in.astype(jnp.bfloat16)
        .reshape(local_e, local_rows, 2, n_mp, quarter)
        .transpose(0, 3, 1, 2, 4)
    )
    out_cast = (
        expert_out.astype(jnp.bfloat16)
        .reshape(local_e, local_rows, n_mp, quarter)
        .transpose(0, 2, 1, 3)
    )
    in_send = in_cast.reshape(local_e * n_mp, local_rows, 2, quarter)
    out_send = out_cast.reshape(local_e * n_mp, local_rows, quarter)
    in_recv, out_recv = (
        lax.all_to_all(in_send, ("expert", "mp"), split_axis=0, concat_axis=1, tiled=True),
        lax.all_to_all(out_send, ("expert", "mp"), split_axis=0, concat_axis=1, tiled=True),
    )
    gate_up_w = in_recv.reshape(width, 2 * quarter)
    down_w = out_recv.reshape(width, quarter)
    normed = rms_scale(hidden, norm_gain)
    levels = gate_levels.astype(jnp.float32)
    gate_weights = levels / jnp.sum(levels, axis=1, keepdims=True)
    flat_ids = expert_ids.reshape(-1)
    pairs = flat_ids.shape[0]
    onehot = (flat_ids[:, None] == jnp.arange(n_groups, dtype=jnp.int32)[None, :]).astype(jnp.int32)
    before = jnp.cumsum(onehot, axis=0) - onehot
    slot_of_pair = jnp.sum(before * onehot, axis=1)
    target = flat_ids * capacity + slot_of_pair
    token_of_pair = jnp.arange(pairs, dtype=jnp.int32) // top
    send = (
        jnp.zeros((n_groups * capacity, width), jnp.bfloat16).at[target].set(normed[token_of_pair])
    )
    received = lax.all_to_all(
        send.reshape(n_groups, capacity, width),
        ("dp", "expert"),
        split_axis=0,
        concat_axis=0,
        tiled=True,
    )
    slots_here = received.reshape(n_groups * capacity, width)
    every_slot = lax.all_gather(slots_here, "mp", axis=0, tiled=True)
    rows = every_slot
    summed = lax.psum_scatter(
        expert_part(rows, gate_up_w, down_w).astype(jnp.bfloat16),
        "mp",
        scatter_dimension=0,
        tiled=True,
    )
    result = summed.reshape(n_groups, capacity, width)
    back = lax.all_to_all(
        result, ("dp", "expert"), split_axis=0, concat_axis=0, tiled=True
    ).reshape(n_groups * capacity, width)
    picked = back[target].reshape(tok_rows, top, width)
    routed = jnp.sum(picked.astype(jnp.float32) * gate_weights[:, :, None], axis=1)
    gate_w, up_w, down_s = (
        lax.all_gather(shared_gate, ("dp", "expert"), axis=0, tiled=True),
        lax.all_gather(shared_up, ("dp", "expert"), axis=0, tiled=True),
        lax.all_gather(shared_down, ("dp", "expert"), axis=0, tiled=True),
    )
    group_rows = lax.all_gather(normed, "mp", axis=0, tiled=True)
    rows = group_rows
    gate_part = jnp.dot(rows, gate_w, preferred_element_type=jnp.float32)
    up_part = jnp.dot(rows, up_w, preferred_element_type=jnp.float32)
    act = (jax.nn.silu(gate_part) * up_part).astype(jnp.bfloat16)
    shared_out = lax.psum_scatter(
        lax.dot_general(act, down_s, (((1,), (1,)), ((), ())), preferred_element_type=jnp.float32),
        "mp",
        scatter_dimension=0,
        tiled=True,
    )
    layer_out = (hidden.astype(jnp.float32) + routed + shared_out).astype(jnp.bfloat16)
    next_rows = rms_scale(layer_out, next_gain)
    next_group = lax.all_gather(next_rows, "mp", axis=0, tiled=True)
    kv_latent = jnp.dot(next_group, kv_weight, preferred_element_type=jnp.float32).astype(
        jnp.bfloat16
    )
    return (layer_out, kv_latent)


def solution(mesh):
    in_specs = (
        P(("dp", "expert", "mp"), None),
        P(),
        P("dp", ("expert", "mp"), None),
        P("dp", ("expert", "mp"), None),
        P(("dp", "expert", "mp"), None),
        P(("dp", "expert", "mp"), None),
        P(("dp", "expert"), "mp"),
        P(("dp", "expert"), "mp"),
        P(("dp", "expert"), "mp"),
        P(),
        P(None, "mp"),
    )
    out_specs = (P(("dp", "expert", "mp"), None), P(("dp", "expert"), "mp"))

    def run(*args):
        dense = dense_fits(mesh, args[0], args[2], args[4])
        return jax.shard_map(
            dense_on_device if dense else on_device,
            mesh=mesh,
            in_specs=in_specs,
            out_specs=out_specs,
            check_vma=False,
        )(*args)

    return run
```
